32 devices in a mesh: heads: 2 (over x), slab: 16 (over z, y, core).
Axes of the slice: x: 2, y: 2, z: 4, core: 2. Of those that a mesh axis runs over, the one named last changes fastest.
Arguments:
- tokens: bfloat16 [16, 384, 3072], P('slab', 'heads'), may hold values from -400 to 400
- qkv_weight: bfloat16 [3072, 4608], P(None, 'heads'), may hold values from -1 to 1
- out_weight: bfloat16 [1536, 3072], P('heads'), may hold values from -0.15625 to 0.15625
- query_gain: float32 [128], replicated, may hold values from 0.6 to 4.5
- key_gain: float32 [128], replicated, may hold values from 0.6 to 4.5
- mod_shift: float32 [3072], replicated, may hold values from -3 to 3
- mod_scale: float32 [3072], replicated, may hold values from -0.5 to 1.5
- branch_gate: float32 [3072], replicated, may hold values from 1 to 3
- block_mask: int32 [16, 27], P('slab'), may hold values 0 or 1
Outputs:
- attended: bfloat16 [16, 384, 3072], P('slab', 'heads')
The draws below stay inside these ranges and needn't reach their ends.
All inputs are finite; a program needn't handle non-finite values. No bound on the sum of `block_mask` on one device may be relied on, other than what follows from the above.
Results may differ from the reference program's by a relative error of at most 0.0095.
The reference program's roundings to bfloat16 on the way count: a program that leaves them out, or rounds other values in their place, can miss the bound.
Values may be sent and summed in bfloat16 or wider, within the bound.
A program may use at most 320 MiB of HBM per device.

```python
import math
import jax
import jax.numpy as jnp
from jax import lax

D = 3072
ATT_HEADS = 12
HD = 128
TILE = 384
GT = 4
GH = 2
GW = 2
TILES = 16
N_HEADS = 2


def draw_tokens(key, part):
    key_base = jax.random.fold_in(key, 1)
    key_rows = jax.random.fold_in(key, 2)
    key_cols = jax.random.fold_in(key, 3)
    row_scale = jnp.exp(jax.random.uniform(key_rows, (TILES, TILE, 1), jnp.float32) * math.log(10.0))
    col_scale = jnp.exp(jax.random.uniform(key_cols, (D,), jnp.float32) * math.log(10.0))
    values_base = jnp.clip(jax.random.normal(key_base, (TILES, TILE, D), jnp.float32), -4.0, 4.0)
    return (values_base * row_scale * col_scale).astype(jnp.bfloat16)


def draw_qkv_weight(key, part):
    values_base = jnp.clip(jax.random.normal(jax.random.fold_in(key, 5), (D, ATT_HEADS, 3, HD), jnp.float32), -5.0, 5.0) * D ** (-0.5)
    return values_base.reshape(D, 3 * ATT_HEADS * HD).astype(jnp.bfloat16)


def draw_query_gain(key, part):
    return jax.random.uniform(jax.random.fold_in(key, 21), (HD,), jnp.float32, 0.6, 2.0)


def draw_key_gain(key, part):
    return jax.random.uniform(jax.random.fold_in(key, 31), (HD,), jnp.float32, 0.6, 2.0)


def plant(array, own_key, low, high):
    longest = array.shape.index(max(array.shape))
    spots = []
    for shift in (0, 1):
        where = [jax.random.randint(jax.random.fold_in(own_key, axis), (), 0, length) for axis, length in enumerate(array.shape)]
        where[longest] = (where[longest] + shift) % array.shape[longest]
        spots.append(tuple(where))
    return array.at[spots[0]].set(low).at[spots[1]].set(high)


def block_scale(stream_key, dims, cuts, low, largest):
    gain = 1.0
    for axis_at, blocks in cuts:
        draws = jax.random.uniform(jax.random.fold_in(jax.random.fold_in(stream_key, 6), axis_at), (blocks,), jnp.float32, low / len(cuts), largest / len(cuts))
        gain = gain * jnp.repeat(jnp.exp(draws), dims[axis_at] // blocks).reshape((-1,) + (1,) * (len(dims) - 1 - axis_at))
    return gain


def normal_values(stream_key, extent, spread, bound, cuts=(), kind=jnp.bfloat16):
    entries = spread * jax.random.normal(stream_key, extent, jnp.float32)
    if cuts:
        entries = entries * block_scale(stream_key, extent, cuts, -0.22, 0.18)
    return jnp.clip(entries, -bound, bound).astype(kind)


def setup_inputs(seed: int = 0) -> dict:
    seeds = jax.random.split(jax.random.key(seed), 10)
    return {
        "tokens": draw_tokens(jax.random.fold_in(seeds[9], 71), 0),
        "qkv_weight": draw_qkv_weight(jax.random.fold_in(seeds[9], 71), 0),
        "out_weight": normal_values(seeds[2], (ATT_HEADS * HD, D), (ATT_HEADS * HD) ** -0.5, 0.15625, ((0, 2),)),
        "query_gain": draw_query_gain(jax.random.fold_in(seeds[9], 71), 0),
        "key_gain": draw_key_gain(jax.random.fold_in(seeds[9], 71), 0),
        "mod_shift": normal_values(seeds[5], (D,), 0.5, 3.0, (), jnp.float32),
        "mod_scale": jnp.clip(jax.random.uniform(seeds[6], (D,), jnp.float32, -0.5, 1.5), -0.5, 1.5),
        "branch_gate": jnp.clip(jax.random.uniform(seeds[7], (D,), jnp.float32, 1.0, 3.0), 1.0, 3.0),
        "block_mask": plant((jax.random.randint(seeds[8], (TILES, 27), 0, 3) < 2).astype(jnp.int32), jax.random.fold_in(seeds[8], 1), 0, 1),
    }


def modulate(token_rows, mod_shift, mod_scale):
    token_rows = token_rows.astype(jnp.float32)
    row_mean = lax.optimization_barrier(jnp.mean(token_rows, axis=-1, keepdims=True))
    centered = token_rows - row_mean
    variance = lax.optimization_barrier(jnp.mean(centered * centered, axis=-1, keepdims=True))
    return (centered * lax.rsqrt(variance + 1e-06) * (1.0 + mod_scale) + mod_shift).astype(jnp.bfloat16)

def head_norm(head_rows, scale_gain):
    head_rows = head_rows.astype(jnp.float32)
    return head_rows * lax.rsqrt(lax.optimization_barrier(jnp.mean(head_rows * head_rows, axis=-1, keepdims=True)) + 1e-06) * scale_gain

def window_live(mask_row, slab_at, grid_t, grid_h, grid_w):
    time_at = slab_at // (grid_h * grid_w)
    height_at = slab_at // grid_w % grid_h
    width_at = slab_at % grid_w
    offsets = jnp.arange(27, dtype=jnp.int32)
    step_t = offsets // 9 - 1
    step_h = offsets // 3 % 3 - 1
    step_w = offsets % 3 - 1
    inside = (time_at + step_t >= 0) & (time_at + step_t < grid_t)
    inside = inside & (height_at + step_h >= 0) & (height_at + step_h < grid_h)
    inside = inside & (width_at + step_w >= 0) & (width_at + step_w < grid_w)
    return inside & ((offsets == 13) | (mask_row == 1))

def soft_weights(scores, live):
    keep = live[None, :, None]
    masked = jnp.where(keep, scores, -1e+30)
    row_top = lax.optimization_barrier(jnp.max(masked, axis=(1, 2), keepdims=True))
    raised = jnp.where(keep, jnp.exp(masked - row_top), 0.0)
    return (raised / lax.optimization_barrier(jnp.sum(raised, axis=(1, 2), keepdims=True))).astype(jnp.bfloat16)

def reference(tokens, qkv_weight, out_weight, query_gain, key_gain, mod_shift, mod_scale, branch_gate, block_mask):
    tile_count = tokens.shape[0]
    tile_tok = tokens.shape[1]
    normed = modulate(tokens, mod_shift, mod_scale)
    projected = jnp.dot(normed.reshape(-1, D), qkv_weight, preferred_element_type=jnp.float32).astype(jnp.bfloat16)
    pieces = projected.reshape(tile_count, tile_tok, ATT_HEADS, 3, HD)
    queries = (head_norm(pieces[:, :, :, 0], query_gain) * HD ** (-0.5)).astype(jnp.bfloat16)
    all_keys = head_norm(pieces[:, :, :, 1], key_gain).astype(jnp.bfloat16)
    all_values = pieces[:, :, :, 2]
    grid_shape = (GT, GH, GW, tile_tok, ATT_HEADS, HD)
    widths = ((1, 1), (1, 1), (1, 1), (0, 0), (0, 0), (0, 0))
    padded_keys = jnp.pad(all_keys.reshape(grid_shape), widths)
    padded_values = jnp.pad(all_values.reshape(grid_shape), widths)

    def one_tile(slab_at):
        time_at = slab_at // (GH * GW)
        height_at = slab_at // GW % GH
        width_at = slab_at % GW
        zero = jnp.zeros((), jnp.int32)
        starts = (time_at, height_at, width_at, zero, zero, zero)
        sizes = (3, 3, 3, tile_tok, ATT_HEADS, HD)
        window_keys = lax.dynamic_slice(padded_keys, starts, sizes).reshape(27, tile_tok, ATT_HEADS, HD)
        window_values = lax.dynamic_slice(padded_values, starts, sizes).reshape(27, tile_tok, ATT_HEADS, HD)
        own_queries = lax.dynamic_index_in_dim(queries, slab_at, 0, keepdims=False)
        mask_row = lax.dynamic_index_in_dim(block_mask, slab_at, 0, keepdims=False)
        live = window_live(mask_row, slab_at, GT, GH, GW)

        def one_head(head_at):
            query_rows = lax.dynamic_index_in_dim(own_queries, head_at, 1, keepdims=False).astype(jnp.float32)
            key_rows = lax.dynamic_index_in_dim(window_keys, head_at, 2, keepdims=False).astype(jnp.float32)
            value_rows = lax.dynamic_index_in_dim(window_values, head_at, 2, keepdims=False).astype(jnp.float32)
            scores = jnp.einsum('qd,okd->qok', query_rows, key_rows)
            weights = soft_weights(scores, live).astype(jnp.float32)
            return jnp.einsum('qok,okd->qd', weights, value_rows).astype(jnp.bfloat16)
        per_head = lax.map(one_head, jnp.arange(ATT_HEADS, dtype=jnp.int32))
        return jnp.transpose(per_head, (1, 0, 2))
    attention = lax.map(one_tile, jnp.arange(tile_count, dtype=jnp.int32))
    flat_rows = attention.reshape(tile_count * tile_tok, ATT_HEADS * HD)
    group_width = ATT_HEADS * HD // N_HEADS
    summed = jnp.zeros((tile_count * tile_tok, D), jnp.float32)
    for group_at in range(N_HEADS):
        lower = group_at * group_width
        term = jnp.dot(flat_rows[:, lower:lower + group_width], out_weight[lower:lower + group_width], preferred_element_type=jnp.float32)
        rounded = lax.optimization_barrier(term.astype(jnp.bfloat16))
        summed = summed + rounded.astype(jnp.float32)
    return (branch_gate * summed).astype(jnp.bfloat16).reshape(tile_count, tile_tok, D)
```

```python
import functools

import jax
import jax.numpy as jnp
from jax import lax
from jax.experimental import pallas as pl
from jax.experimental.pallas import tpu as pltpu
from jax.sharding import PartitionSpec as P

GT = 4
MESH = pl.DeviceIdType.MESH
PAIR = 2


def slots_of(size):
    return 2 if size == 2 else 3


def moves(size, pos):
    if size == 2:
        return [(1, 1 - pos, None)]
    return [(1, pos + 1, pos + 1 < size), (2, pos - 1, pos > 0)]


def has(size, pos, place):
    if place == 0 or size == 2:
        return None
    return pos > 0 if place == 1 else pos + 1 < size


def both(first, second):
    if first is None:
        return second
    if second is None:
        return first
    return jnp.logical_and(first, second)


def guarded(cond, run):
    if cond is None:
        run()
    else:
        pl.when(cond)(run)


def normed_rows(rows, shift, scale):
    rows = rows.astype(jnp.float32)
    centered = rows - jnp.mean(rows, axis=-1, keepdims=True)
    variance = jnp.mean(centered * centered, axis=-1, keepdims=True)
    return (centered * lax.rsqrt(variance + 1e-06) * (1.0 + scale) + shift).astype(jnp.bfloat16)


def head_norm(rows, gain):
    rows = rows.astype(jnp.float32)
    return rows * lax.rsqrt(jnp.mean(rows * rows, axis=-1, keepdims=True) + 1e-06) * gain


def gather_kernel(
    grid, tokens, weight, qgain, kgain, shift, scale, win, q_out,
    nx, wbuf, kv, wsem, xsend, xrecv, ssem, rsem, lsem,
):
    size_t, size_h, size_w = grid
    num_h, num_w = slots_of(size_h), slots_of(size_w)
    num_t = slots_of(size_t)
    pairs = wbuf.shape[0]
    rows = tokens.shape[0]
    hd = qgain.shape[1]
    pair_cols = wbuf.shape[2]
    me_x = lax.axis_index("heads")
    me = lax.axis_index("slab")
    at_t = me // (size_h * size_w)
    at_h = me // size_w % size_h
    at_w = me % size_w

    def device(t, h, w):
        return (me_x, (t * size_h + h) * size_w + w)

    def slot(a, b, c):
        return (a * num_h + b) * num_w + c

    for p in range(pairs):
        pltpu.make_async_copy(
            weight.at[:, pl.ds(p * pair_cols, pair_cols)], wbuf.at[p], wsem.at[p]
        ).start()

    barrier = pltpu.get_barrier_semaphore()
    near = [(None, (1 - me_x, me))]
    near += [(ok, device(n, at_h, at_w)) for _, n, ok in moves(size_t, at_t)]
    near += [(ok, device(at_t, n, at_w)) for _, n, ok in moves(size_h, at_h)]
    near += [(ok, device(at_t, at_h, n)) for _, n, ok in moves(size_w, at_w)]
    for ok, target in near:
        guarded(
            ok,
            lambda target=target: pl.semaphore_signal(
                barrier, inc=1, device_id=target, device_id_type=MESH
            ),
        )
    peers = sum(1 if ok is None else ok.astype(jnp.int32) for ok, _ in near)
    pl.semaphore_wait(barrier, peers)

    parts = xsend.shape[0]
    step = rows // parts

    def xcopy(i):
        span = pl.ds(i * step, step)
        return pltpu.make_async_remote_copy(
            src_ref=nx.at[0, span], dst_ref=nx.at[1, span],
            send_sem=xsend.at[i], recv_sem=xrecv.at[i],
            device_id=(1 - me_x, me), device_id_type=MESH,
        )

    for i in range(parts):
        def norm_step(j, carry, i=i):
            span = pl.ds(pl.multiple_of(i * step + j * 16, 16), 16)
            nx[0, span, :] = normed_rows(tokens[span, :], shift[...], scale[...])
            return carry

        lax.fori_loop(0, step // 16, norm_step, 0)
        xcopy(i).start()

    def chunk(ref, half, p):
        return ref.at[half, pl.ds(p * PAIR, PAIR)]

    def local(half, p):
        return pltpu.make_async_copy(
            chunk(kv, half, p), chunk(win.at[0], half, p), lsem.at[half, p]
        )

    def remote(half, p, src, dst, target):
        at = half * pairs + p
        source = chunk(kv, half, p) if src == 0 else chunk(win.at[src], half, p)
        return pltpu.make_async_remote_copy(
            src_ref=source, dst_ref=chunk(win.at[dst], half, p),
            send_sem=ssem.at[at, dst], recv_sem=rsem.at[at, dst],
            device_id=target, device_id_type=MESH,
        )

    def along_t(b):
        return [
            (both(ok, has(size_h, at_h, b)), slot(0, b, 0), slot(a, b, 0), device(n, at_h, at_w))
            for a, n, ok in moves(size_t, at_t)
        ]

    def along_h(a):
        return [
            (both(ok, has(size_t, at_t, a)), slot(a, 0, 0), slot(a, b, 0), device(at_t, n, at_w))
            for b, n, ok in moves(size_h, at_h)
        ]

    def along_w(a, b):
        here = both(has(size_t, at_t, a), has(size_h, at_h, b))
        return [
            (both(ok, here), slot(a, b, 0), slot(a, b, c), device(at_t, at_h, n))
            for c, n, ok in moves(size_w, at_w)
        ]

    def start(half, p, sends):
        for ok, src, dst, target in sends:
            guarded(
                ok,
                lambda src=src, dst=dst, target=target: remote(half, p, src, dst, target).start(),
            )

    def await_sent(half, p, sends):
        for ok, src, dst, target in sends:
            guarded(
                ok,
                lambda src=src, dst=dst, target=target: remote(
                    half, p, src, dst, target
                ).wait_send(),
            )

    def await_place(half, p, a, b, c):
        ok = both(both(has(size_t, at_t, a), has(size_h, at_h, b)), has(size_w, at_w, c))
        spot = slot(a, b, c)
        guarded(ok, lambda: remote(half, p, 0, spot, (1 - me_x, me)).wait_recv())

    def time_first(p):
        return p == pairs - 1

    def first(half, p):
        local(half, p).start()
        start(half, p, along_h(0) + along_t(0) + along_w(0, 0))

    def second(half, p):
        for a in range(1, num_t):
            if not time_first(p):
                break
            await_place(half, p, a, 0, 0)
            start(half, p, along_h(a))
        for b in range(1, num_h):
            if time_first(p):
                break
            await_place(half, p, 0, b, 0)
            start(half, p, along_t(b))

    def third(half, p):
        for a in range(num_t):
            for b in range(num_h):
                if a == 0 and b == 0:
                    continue
                waited = (time_first(p) and b == 0) or (not time_first(p) and a == 0)
                if not waited:
                    await_place(half, p, a, b, 0)
                else:
                    continue
                start(half, p, along_w(a, b))

    def early(half, p):
        if time_first(p):
            for a in range(1, num_t):
                start(half, p, along_w(a, 0))
        else:
            for b in range(1, num_h):
                start(half, p, along_w(0, b))

    def finish(half, p):
        for a in range(num_t):
            for b in range(num_h):
                for c in range(1, num_w):
                    await_place(half, p, a, b, c)
        sends = along_t(0) + along_h(0)
        if time_first(p):
            for a in range(1, num_t):
                sends += along_h(a)
        else:
            for b in range(1, num_h):
                sends += along_t(b)
        for a in range(num_t):
            for b in range(num_h):
                sends += along_w(a, b)
        await_sent(half, p, sends)
        local(half, p).wait()

    def project(half, p):
        out = jnp.dot(
            nx[half], wbuf[p], preferred_element_type=jnp.float32
        ).astype(jnp.bfloat16)
        for i in range(PAIR):
            base = i * 3 * hd
            query = head_norm(out[:, base:base + hd], qgain[...]) * hd ** (-0.5)
            q_out[half, p * PAIR + i] = query.astype(jnp.bfloat16)
            key = head_norm(out[:, base + hd:base + 2 * hd], kgain[...])
            kv[half, p * PAIR + i, 0] = key.astype(jnp.bfloat16)
            kv[half, p * PAIR + i, 1] = out[:, base + 2 * hd:base + 3 * hd]

    for p in range(pairs):
        pltpu.make_async_copy(
            weight.at[:, pl.ds(p * pair_cols, pair_cols)], wbuf.at[p], wsem.at[p]
        ).wait()
        project(0, p)
        first(0, p)
    for p in range(pairs):
        second(0, p)
        early(0, p)
    for i in range(parts):
        xcopy(i).wait_recv()
    for p in range(pairs):
        project(1, p)
        first(1, p)
    for p in range(pairs):
        third(0, p)
    for p in range(pairs):
        second(1, p)
        early(1, p)
    for p in range(pairs):
        third(1, p)
    for half in range(2):
        for p in range(pairs):
            finish(half, p)
    for i in range(parts):
        xcopy(i).wait_send()


def attend_kernel(places, count, q_ref, win_ref, out_ref):
    q = jnp.concatenate([q_ref[0, 0], q_ref[1, 0]], axis=0)
    rows, hd = q.shape

    def step(i, carry):
        top, total, acc = carry
        spot = places[i]
        k = jnp.concatenate([win_ref[spot, 0, 0, 0], win_ref[spot, 1, 0, 0]], axis=0)
        v = jnp.concatenate([win_ref[spot, 0, 0, 1], win_ref[spot, 1, 0, 1]], axis=0)
        s = lax.dot_general(q, k, (((1,), (1,)), ((), ())), preferred_element_type=jnp.float32)
        new_top = jnp.maximum(top, jnp.max(s, axis=1, keepdims=True))
        fade = jnp.exp(top - new_top)
        raised = jnp.exp(s - new_top)
        total = total * fade + jnp.sum(raised, axis=1, keepdims=True)
        acc = acc * fade + jnp.dot(
            raised.astype(jnp.bfloat16), v, preferred_element_type=jnp.float32
        )
        return new_top, total, acc

    init = (
        jnp.full((rows, 1), -1e30, jnp.float32),
        jnp.zeros((rows, 1), jnp.float32),
        jnp.zeros((rows, hd), jnp.float32),
    )
    _, total, acc = lax.fori_loop(0, count[0], step, init)
    result = (acc / total).astype(jnp.bfloat16)
    out_ref[0] = result[: rows // 2]
    out_ref[1] = result[rows // 2:]


def output_kernel(att, weight, gate, out, sendbuf, recvbuf, ssem, rsem):
    me_x = lax.axis_index("heads")
    me = lax.axis_index("slab")
    peer = (1 - me_x, me)
    parts = sendbuf.shape[0]
    width = sendbuf.shape[2]
    barrier = pltpu.get_barrier_semaphore()
    pl.semaphore_signal(barrier, inc=1, device_id=peer, device_id_type=MESH)
    pl.semaphore_wait(barrier, 1)

    def copy(i):
        return pltpu.make_async_remote_copy(
            src_ref=sendbuf.at[i], dst_ref=recvbuf.at[i],
            send_sem=ssem.at[i], recv_sem=rsem.at[i],
            device_id=peer, device_id_type=MESH,
        )

    for i in range(parts):
        cols = slice(i * width, (i + 1) * width)
        sendbuf[i] = jnp.dot(
            att[1], weight[:, cols], preferred_element_type=jnp.float32
        ).astype(jnp.bfloat16)
        copy(i).start()
    for i in range(parts):
        cols = slice(i * width, (i + 1) * width)
        own = jnp.dot(att[0], weight[:, cols], preferred_element_type=jnp.float32).astype(
            jnp.bfloat16
        )
        copy(i).wait_recv()
        summed = own.astype(jnp.float32) + recvbuf[i].astype(jnp.float32)
        out[0, :, cols] = (gate[:, cols] * summed).astype(jnp.bfloat16)
    for i in range(parts):
        copy(i).wait_send()


def live_places(mask_row, grid):
    size_t, size_h, size_w = grid
    me = lax.axis_index("slab")
    pos = (me // (size_h * size_w), me // size_w % size_h, me % size_w)

    def offsets(size, at):
        if size == 2:
            return [0 * at, 1 - 2 * at]
        return [0 * at, 0 * at - 1, 0 * at + 1]

    orders, inside = [], []
    for dt in offsets(size_t, pos[0]):
        for dh in offsets(size_h, pos[1]):
            for dw in offsets(size_w, pos[2]):
                orders.append(9 * (dt + 1) + 3 * (dh + 1) + dw + 1)
                ok = True
                for at, delta, size in zip(pos, (dt, dh, dw), grid):
                    ok = ok & (at + delta >= 0) & (at + delta < size)
                inside.append(ok)
    order = jnp.stack(orders)
    chosen = (order[:, None] == jnp.arange(27)[None]) & (mask_row[None] == 1)
    live = jnp.stack(inside) & ((order == 13) | jnp.any(chosen, axis=1))
    amount = order.shape[0]
    ids = jnp.arange(amount, dtype=jnp.int32)
    rank = jnp.sum((ids[None] < ids[:, None]) & live[None], axis=1)
    hit = live[:, None] & (rank[:, None] == ids[None])
    places = jnp.sum(jnp.where(hit, ids[:, None], 0), axis=0).astype(jnp.int32)
    return places, jnp.sum(live.astype(jnp.int32)).reshape(1)


def on_device(
    tokens, qkv_weight, out_weight, query_gain, key_gain, mod_shift, mod_scale, branch_gate,
    block_mask,
):
    hd = query_gain.shape[0]
    group_width = out_weight.shape[0]
    heads = group_width // hd
    rows, model = tokens.shape[1:]
    pairs = heads // PAIR
    slab_count = lax.axis_size("slab")
    size_h = min(4, slab_count // 8)
    grid = (GT, size_h, slab_count // (GT * size_h))
    places = slots_of(grid[0]) * slots_of(grid[1]) * slots_of(grid[2])
    vmem = pl.BlockSpec(memory_space=pltpu.VMEM)
    anywhere = pl.BlockSpec(memory_space=pl.ANY)
    bf16 = jnp.bfloat16
    win, queries = pl.pallas_call(
        functools.partial(gather_kernel, grid),
        out_shape=(
            jax.ShapeDtypeStruct((places, 2, heads, 2, rows, hd), bf16),
            jax.ShapeDtypeStruct((2, heads, rows, hd), bf16),
        ),
        in_specs=[vmem, anywhere, vmem, vmem, vmem, vmem],
        out_specs=(anywhere, vmem),
        scratch_shapes=[
            pltpu.VMEM((2, rows, model), bf16),
            pltpu.VMEM((pairs, model, 3 * PAIR * hd), bf16),
            pltpu.VMEM((2, heads, 2, rows, hd), bf16),
            pltpu.SemaphoreType.DMA((pairs,)),
            pltpu.SemaphoreType.DMA((2,)),
            pltpu.SemaphoreType.DMA((2,)),
            pltpu.SemaphoreType.DMA((2 * pairs, places)),
            pltpu.SemaphoreType.DMA((2 * pairs, places)),
            pltpu.SemaphoreType.DMA((2, pairs)),
        ],
        compiler_params=pltpu.CompilerParams(
            collective_id=0, has_side_effects=True, vmem_limit_bytes=40 * 2**20
        ),
    )(
        tokens[0], qkv_weight, query_gain[None], key_gain[None], mod_shift[None], mod_scale[None]
    )
    spots, count = live_places(block_mask[0], grid)
    attention = pl.pallas_call(
        attend_kernel,
        grid_spec=pltpu.PrefetchScalarGridSpec(
            num_scalar_prefetch=2,
            grid=(heads,),
            in_specs=[
                pl.BlockSpec((2, 1, rows, hd), lambda h, *_: (0, h, 0, 0)),
                pl.BlockSpec((places, 2, 1, 2, rows, hd), lambda h, *_: (0, 0, h, 0, 0, 0)),
            ],
            out_specs=pl.BlockSpec((2, rows, hd), lambda h, *_: (0, 0, h)),
        ),
        out_shape=jax.ShapeDtypeStruct((2, rows, group_width), bf16),
        compiler_params=pltpu.CompilerParams(vmem_limit_bytes=40 * 2**20),
    )(spots, count, queries, win)
    parts = 4
    return pl.pallas_call(
        output_kernel,
        out_shape=jax.ShapeDtypeStruct((1, rows, model), bf16),
        in_specs=[vmem, vmem, vmem],
        out_specs=vmem,
        scratch_shapes=[
            pltpu.VMEM((parts, rows, model // parts), bf16),
            pltpu.VMEM((parts, rows, model // parts), bf16),
            pltpu.SemaphoreType.DMA((parts,)),
            pltpu.SemaphoreType.DMA((parts,)),
        ],
        compiler_params=pltpu.CompilerParams(
            collective_id=1, has_side_effects=True, vmem_limit_bytes=40 * 2**20
        ),
    )(attention, out_weight, branch_gate[None])


def solution(mesh):
    in_specs = (
        P("slab", "heads", None),
        P(None, "heads"),
        P("heads", None),
        P(),
        P(),
        P(),
        P(),
        P(),
        P("slab", None),
    )
    return jax.shard_map(
        on_device, mesh=mesh, in_specs=in_specs, out_specs=P("slab", "heads", None),
        check_vma=False,
    )
```

```python
import functools

import jax
import jax.numpy as jnp
from jax import lax
from jax.experimental import pallas as pl
from jax.experimental.pallas import tpu as pltpu
from jax.sharding import PartitionSpec as P

GT = 4
MESH = pl.DeviceIdType.MESH
PAIR = 2


def slots_of(size):
    return 2 if size == 2 else 3


def moves(size, pos):
    if size == 2:
        return [(1, 1 - pos, None)]
    return [(1, pos + 1, pos + 1 < size), (2, pos - 1, pos > 0)]


def has(size, pos, place):
    if place == 0 or size == 2:
        return None
    return pos > 0 if place == 1 else pos + 1 < size


def both(first, second):
    if first is None:
        return second
    if second is None:
        return first
    return jnp.logical_and(first, second)


def guarded(cond, run):
    if cond is None:
        run()
    else:
        pl.when(cond)(run)


def normed_rows(rows, shift, scale):
    rows = rows.astype(jnp.float32)
    centered = rows - jnp.mean(rows, axis=-1, keepdims=True)
    variance = jnp.mean(centered * centered, axis=-1, keepdims=True)
    return (centered * lax.rsqrt(variance + 1e-06) * (1.0 + scale) + shift).astype(jnp.bfloat16)


def head_norm(rows, gain):
    rows = rows.astype(jnp.float32)
    return rows * lax.rsqrt(jnp.mean(rows * rows, axis=-1, keepdims=True) + 1e-06) * gain


def gather_kernel(
    grid, tokens, weight, qgain, kgain, shift, scale, win, q_out,
    nx, wbuf, kv, wsem, xsend, xrecv, ssem, rsem, lsem,
):
    size_t, size_h, size_w = grid
    num_h, num_w = slots_of(size_h), slots_of(size_w)
    num_t = slots_of(size_t)
    pairs = wbuf.shape[0]
    rows = tokens.shape[0]
    hd = qgain.shape[1]
    pair_cols = wbuf.shape[2]
    me_x = lax.axis_index("heads")
    me = lax.axis_index("slab")
    at_t = me // (size_h * size_w)
    at_h = me // size_w % size_h
    at_w = me % size_w

    def device(t, h, w):
        return (me_x, (t * size_h + h) * size_w + w)

    def slot(a, b, c):
        return (a * num_h + b) * num_w + c

    for p in range(pairs):
        pltpu.make_async_copy(
            weight.at[:, pl.ds(p * pair_cols, pair_cols)], wbuf.at[p], wsem.at[p]
        ).start()

    barrier = pltpu.get_barrier_semaphore()
    near = [(None, (1 - me_x, me))]
    near += [(ok, device(n, at_h, at_w)) for _, n, ok in moves(size_t, at_t)]
    near += [(ok, device(at_t, n, at_w)) for _, n, ok in moves(size_h, at_h)]
    near += [(ok, device(at_t, at_h, n)) for _, n, ok in moves(size_w, at_w)]
    for ok, target in near:
        guarded(
            ok,
            lambda target=target: pl.semaphore_signal(
                barrier, inc=1, device_id=target, device_id_type=MESH
            ),
        )
    peers = sum(1 if ok is None else ok.astype(jnp.int32) for ok, _ in near)
    pl.semaphore_wait(barrier, peers)

    parts = xsend.shape[0]
    step = rows // parts

    def xcopy(i):
        span = pl.ds(i * step, step)
        return pltpu.make_async_remote_copy(
            src_ref=nx.at[0, span], dst_ref=nx.at[1, span],
            send_sem=xsend.at[i], recv_sem=xrecv.at[i],
            device_id=(1 - me_x, me), device_id_type=MESH,
        )

    for i in range(parts):
        def norm_step(j, carry, i=i):
            span = pl.ds(pl.multiple_of(i * step + j * 16, 16), 16)
            nx[0, span, :] = normed_rows(tokens[span, :], shift[...], scale[...])
            return carry

        lax.fori_loop(0, step // 16, norm_step, 0)
        xcopy(i).start()

    def chunk(ref, half, p):
        return ref.at[half, pl.ds(p * PAIR, PAIR)]

    def local(half, p):
        return pltpu.make_async_copy(
            chunk(kv, half, p), chunk(win.at[0], half, p), lsem.at[half, p]
        )

    def remote(half, p, src, dst, target):
        at = half * pairs + p
        source = chunk(kv, half, p) if src == 0 else chunk(win.at[src], half, p)
        return pltpu.make_async_remote_copy(
            src_ref=source, dst_ref=chunk(win.at[dst], half, p),
            send_sem=ssem.at[at, dst], recv_sem=rsem.at[at, dst],
            device_id=target, device_id_type=MESH,
        )

    def along_t(b):
        return [
            (both(ok, has(size_h, at_h, b)), slot(0, b, 0), slot(a, b, 0), device(n, at_h, at_w))
            for a, n, ok in moves(size_t, at_t)
        ]

    def along_h(a):
        return [
            (both(ok, has(size_t, at_t, a)), slot(a, 0, 0), slot(a, b, 0), device(at_t, n, at_w))
            for b, n, ok in moves(size_h, at_h)
        ]

    def along_w(a, b):
        here = both(has(size_t, at_t, a), has(size_h, at_h, b))
        return [
            (both(ok, here), slot(a, b, 0), slot(a, b, c), device(at_t, at_h, n))
            for c, n, ok in moves(size_w, at_w)
        ]

    def start(half, p, sends):
        for ok, src, dst, target in sends:
            guarded(
                ok,
                lambda src=src, dst=dst, target=target: remote(half, p, src, dst, target).start(),
            )

    def await_sent(half, p, sends):
        for ok, src, dst, target in sends:
            guarded(
                ok,
                lambda src=src, dst=dst, target=target: remote(
                    half, p, src, dst, target
                ).wait_send(),
            )

    def await_place(half, p, a, b, c):
        ok = both(both(has(size_t, at_t, a), has(size_h, at_h, b)), has(size_w, at_w, c))
        spot = slot(a, b, c)
        guarded(ok, lambda: remote(half, p, 0, spot, (1 - me_x, me)).wait_recv())

    def time_first(p):
        return p == pairs - 1

    def first(half, p):
        local(half, p).start()
        start(half, p, along_h(0) + along_t(0) + along_w(0, 0))

    def second(half, p):
        for a in range(1, num_t):
            if not time_first(p):
                break
            await_place(half, p, a, 0, 0)
            start(half, p, along_h(a))
        for b in range(1, num_h):
            if time_first(p):
                break
            await_place(half, p, 0, b, 0)
            start(half, p, along_t(b))

    def third(half, p):
        for a in range(num_t):
            for b in range(num_h):
                if a == 0 and b == 0:
                    continue
                waited = (time_first(p) and b == 0) or (not time_first(p) and a == 0)
                if not waited:
                    await_place(half, p, a, b, 0)
                else:
                    continue
                start(half, p, along_w(a, b))

    def early(half, p):
        if time_first(p):
            for a in range(1, num_t):
                start(half, p, along_w(a, 0))
        else:
            for b in range(1, num_h):
                start(half, p, along_w(0, b))

    def finish(half, p):
        for a in range(num_t):
            for b in range(num_h):
                for c in range(1, num_w):
                    await_place(half, p, a, b, c)
        sends = along_t(0) + along_h(0)
        if time_first(p):
            for a in range(1, num_t):
                sends += along_h(a)
        else:
            for b in range(1, num_h):
                sends += along_t(b)
        for a in range(num_t):
            for b in range(num_h):
                sends += along_w(a, b)
        await_sent(half, p, sends)
        local(half, p).wait()

    def project(half, p):
        out = jnp.dot(
            nx[half], wbuf[p], preferred_element_type=jnp.float32
        ).astype(jnp.bfloat16)
        for i in range(PAIR):
            base = i * 3 * hd
            query = head_norm(out[:, base:base + hd], qgain[...]) * hd ** (-0.5)
            q_out[half, p * PAIR + i] = query.astype(jnp.bfloat16)
            key = head_norm(out[:, base + hd:base + 2 * hd], kgain[...])
            kv[half, p * PAIR + i, 0] = key.astype(jnp.bfloat16)
            kv[half, p * PAIR + i, 1] = out[:, base + 2 * hd:base + 3 * hd]

    for p in range(pairs):
        pltpu.make_async_copy(
            weight.at[:, pl.ds(p * pair_cols, pair_cols)], wbuf.at[p], wsem.at[p]
        ).wait()
        project(0, p)
        first(0, p)
    for p in range(pairs):
        second(0, p)
        early(0, p)
    for i in range(parts):
        xcopy(i).wait_recv()
    for p in range(pairs):
        project(1, p)
        first(1, p)
    for p in range(pairs):
        third(0, p)
    for p in range(pairs):
        second(1, p)
        early(1, p)
    for p in range(pairs):
        third(1, p)
    for half in range(2):
        for p in range(pairs):
            finish(half, p)
    for i in range(parts):
        xcopy(i).wait_send()


def attend_kernel(places, count, q_ref, win_ref, weight, out_ref, att, sbuf):
    head = pl.program_id(0)
    q = q_ref[0, 0]
    rows, hd = q.shape
    heads = att.shape[0]
    keys = sbuf.shape[2]
    groups = keys // hd
    trips = (count[0] + 1) // 2

    def both_tiles(i, part):
        return jnp.concatenate(
            [win_ref[places[2 * i + j], half, 0, part] for j in range(2) for half in range(2)],
            axis=0,
        )

    def score(i, top):
        k = both_tiles(i, 0)
        s = lax.dot_general(q, k, (((1,), (1,)), ((), ())), preferred_element_type=jnp.float32)
        ahead, behind = s[:, : keys // 2], s[:, keys // 2:]
        behind = jnp.where(2 * i + 1 < count[0], behind, -1e30)
        sbuf[i, :, : keys // 2] = ahead
        sbuf[i, :, keys // 2:] = behind
        for part in (ahead, behind):
            for g in range(groups // 2):
                top = jnp.maximum(top, part[:, g * hd:(g + 1) * hd])
        return top

    top = lax.fori_loop(0, trips, score, jnp.full((rows, hd), -1e30, jnp.float32))
    top = jnp.max(top, axis=1, keepdims=True)

    def gather(i, carry):
        total, acc = carry
        raised = jnp.exp(sbuf[i] - top)
        for g in range(groups):
            total = total + raised[:, g * hd:(g + 1) * hd]
        acc = acc + jnp.dot(
            raised.astype(jnp.bfloat16), both_tiles(i, 1), preferred_element_type=jnp.float32
        )
        return total, acc

    zero = jnp.zeros((rows, hd), jnp.float32)
    total, acc = lax.fori_loop(0, trips, gather, (zero, zero))
    att[head] = (acc / jnp.sum(total, axis=1, keepdims=True)).astype(jnp.bfloat16)

    @pl.when(head == heads - 1)
    def _():
        full = jnp.concatenate([att[h] for h in range(heads)], axis=1)
        width = weight.shape[1] // 4
        for i in range(4):
            cols = slice(i * width, (i + 1) * width)
            out_ref[:, cols] = jnp.dot(
                full, weight[:, cols], preferred_element_type=jnp.float32
            ).astype(jnp.bfloat16)


def live_places(mask_row, grid):
    size_t, size_h, size_w = grid
    me = lax.axis_index("slab")
    pos = (me // (size_h * size_w), me // size_w % size_h, me % size_w)

    def offsets(size, at):
        if size == 2:
            return [0 * at, 1 - 2 * at]
        return [0 * at, 0 * at - 1, 0 * at + 1]

    orders, inside = [], []
    for dt in offsets(size_t, pos[0]):
        for dh in offsets(size_h, pos[1]):
            for dw in offsets(size_w, pos[2]):
                orders.append(9 * (dt + 1) + 3 * (dh + 1) + dw + 1)
                ok = True
                for at, delta, size in zip(pos, (dt, dh, dw), grid):
                    ok = ok & (at + delta >= 0) & (at + delta < size)
                inside.append(ok)
    order = jnp.stack(orders)
    chosen = (order[:, None] == jnp.arange(27)[None]) & (mask_row[None] == 1)
    live = jnp.stack(inside) & ((order == 13) | jnp.any(chosen, axis=1))
    amount = order.shape[0]
    ids = jnp.arange(amount, dtype=jnp.int32)
    rank = jnp.sum((ids[None] < ids[:, None]) & live[None], axis=1)
    hit = live[:, None] & (rank[:, None] == ids[None])
    places = jnp.sum(jnp.where(hit, ids[:, None], 0), axis=0).astype(jnp.int32)
    return places, jnp.sum(live.astype(jnp.int32)).reshape(1)


def on_device(
    tokens, qkv_weight, out_weight, query_gain, key_gain, mod_shift, mod_scale, branch_gate,
    block_mask,
):
    hd = query_gain.shape[0]
    group_width = out_weight.shape[0]
    heads = group_width // hd
    rows, model = tokens.shape[1:]
    pairs = heads // PAIR
    slab_count = lax.axis_size("slab")
    size_h = min(4, slab_count // 8)
    grid = (GT, size_h, slab_count // (GT * size_h))
    places = slots_of(grid[0]) * slots_of(grid[1]) * slots_of(grid[2])
    vmem = pl.BlockSpec(memory_space=pltpu.VMEM)
    anywhere = pl.BlockSpec(memory_space=pl.ANY)
    bf16 = jnp.bfloat16
    win, queries = pl.pallas_call(
        functools.partial(gather_kernel, grid),
        out_shape=(
            jax.ShapeDtypeStruct((places, 2, heads, 2, rows, hd), bf16),
            jax.ShapeDtypeStruct((2, heads, rows, hd), bf16),
        ),
        in_specs=[vmem, anywhere, vmem, vmem, vmem, vmem],
        out_specs=(anywhere, vmem),
        scratch_shapes=[
            pltpu.VMEM((2, rows, model), bf16),
            pltpu.VMEM((pairs, model, 3 * PAIR * hd), bf16),
            pltpu.VMEM((2, heads, 2, rows, hd), bf16),
            pltpu.SemaphoreType.DMA((pairs,)),
            pltpu.SemaphoreType.DMA((2,)),
            pltpu.SemaphoreType.DMA((2,)),
            pltpu.SemaphoreType.DMA((2 * pairs, places)),
            pltpu.SemaphoreType.DMA((2 * pairs, places)),
            pltpu.SemaphoreType.DMA((2, pairs)),
        ],
        compiler_params=pltpu.CompilerParams(
            collective_id=0, has_side_effects=True, vmem_limit_bytes=40 * 2**20
        ),
    )(
        tokens[0], qkv_weight, query_gain[None], key_gain[None], mod_shift[None], mod_scale[None]
    )
    spots, count = live_places(block_mask[0], grid)
    spots = jnp.concatenate([spots, jnp.zeros((2,), jnp.int32)])
    trips = (places + 1) // 2

    def attend(half, window):
        return pl.pallas_call(
            attend_kernel,
            grid_spec=pltpu.PrefetchScalarGridSpec(
                num_scalar_prefetch=2,
                grid=(heads,),
                in_specs=[
                    pl.BlockSpec((1, 1, rows, hd), lambda h, *_: (half, h, 0, 0)),
                    pl.BlockSpec((places, 2, 1, 2, rows, hd), lambda h, *_: (0, 0, h, 0, 0, 0)),
                    vmem,
                ],
                out_specs=pl.BlockSpec((rows, model), lambda h, *_: (0, 0)),
                scratch_shapes=[
                    pltpu.VMEM((heads, rows, hd), bf16),
                    pltpu.VMEM((trips, rows, 4 * rows), jnp.float32),
                ],
            ),
            out_shape=jax.ShapeDtypeStruct((rows, model), bf16),
            compiler_params=pltpu.CompilerParams(vmem_limit_bytes=44 * 2**20),
            cost_estimate=pl.CostEstimate(
                flops=20 * 10**9, bytes_accessed=20 * 10**6, transcendentals=5 * 10**6
            ),
        )(spots, count, queries, window, out_weight)

    for_peer = attend(1, win)
    for_peer, later = lax.optimization_barrier((for_peer, win))
    from_peer = lax.ppermute(for_peer, "heads", [(0, 1), (1, 0)])
    own = attend(0, later)
    summed = own.astype(jnp.float32) + from_peer.astype(jnp.float32)
    return (branch_gate * summed).astype(bf16)[None]


def solution(mesh):
    in_specs = (
        P("slab", "heads", None),
        P(None, "heads"),
        P("heads", None),
        P(),
        P(),
        P(),
        P(),
        P(),
        P("slab", None),
    )
    return jax.shard_map(
        on_device, mesh=mesh, in_specs=in_specs, out_specs=P("slab", "heads", None),
        check_vma=False,
    )
```

```python
import functools

import jax
import jax.numpy as jnp
from jax import lax
from jax.experimental import pallas as pl
from jax.experimental.pallas import tpu as pltpu
from jax.sharding import PartitionSpec as P

GT = 4
MESH = pl.DeviceIdType.MESH
PAIR = 2


def slots_of(size):
    return 2 if size == 2 else 3


def moves(size, pos):
    if size == 2:
        return [(1, 1 - pos, None)]
    return [(1, pos + 1, pos + 1 < size), (2, pos - 1, pos > 0)]


def has(size, pos, place):
    if place == 0 or size == 2:
        return None
    return pos > 0 if place == 1 else pos + 1 < size


def both(first, second):
    if first is None:
        return second
    if second is None:
        return first
    return jnp.logical_and(first, second)


def guarded(cond, run):
    if cond is None:
        run()
    else:
        pl.when(cond)(run)


def normed_rows(rows, shift, scale):
    rows = rows.astype(jnp.float32)
    centered = rows - jnp.mean(rows, axis=-1, keepdims=True)
    variance = jnp.mean(centered * centered, axis=-1, keepdims=True)
    return (centered * lax.rsqrt(variance + 1e-06) * (1.0 + scale) + shift).astype(jnp.bfloat16)


def head_norm(rows, gain):
    rows = rows.astype(jnp.float32)
    return rows * lax.rsqrt(jnp.mean(rows * rows, axis=-1, keepdims=True) + 1e-06) * gain


def gather_kernel(
    grid, tokens_hbm, weight, qgain_hbm, kgain_hbm, shift_hbm, scale_hbm, win, q_out,
    tokens, qgain, kgain, shift, scale, nx, wbuf, kv, isem, wsem, xsend, xrecv, ssem, rsem, lsem,
):
    size_t, size_h, size_w = grid
    num_h, num_w = slots_of(size_h), slots_of(size_w)
    num_t = slots_of(size_t)
    pairs = wbuf.shape[0]
    rows = tokens.shape[0]
    hd = qgain.shape[1]
    pair_cols = wbuf.shape[2]
    me_x = lax.axis_index("heads")
    me = lax.axis_index("slab")
    at_t = me // (size_h * size_w)
    at_h = me // size_w % size_h
    at_w = me % size_w

    def device(t, h, w):
        return (me_x, (t * size_h + h) * size_w + w)

    def slot(a, b, c):
        return (a * num_h + b) * num_w + c

    loads = [
        pltpu.make_async_copy(src, dst, isem.at[i])
        for i, (src, dst) in enumerate([
            (tokens_hbm, tokens), (shift_hbm, shift), (scale_hbm, scale),
            (qgain_hbm, qgain), (kgain_hbm, kgain),
        ])
    ]
    for load in loads:
        load.start()
    for p in range(pairs):
        pltpu.make_async_copy(
            weight.at[:, pl.ds(p * pair_cols, pair_cols)], wbuf.at[p], wsem.at[p]
        ).start()

    barrier = pltpu.get_barrier_semaphore()
    near = [(None, (1 - me_x, me))]
    near += [(ok, device(n, at_h, at_w)) for _, n, ok in moves(size_t, at_t)]
    near += [(ok, device(at_t, n, at_w)) for _, n, ok in moves(size_h, at_h)]
    near += [(ok, device(at_t, at_h, n)) for _, n, ok in moves(size_w, at_w)]
    for ok, target in near:
        guarded(
            ok,
            lambda target=target: pl.semaphore_signal(
                barrier, inc=1, device_id=target, device_id_type=MESH
            ),
        )
    peers = sum(1 if ok is None else ok.astype(jnp.int32) for ok, _ in near)
    pl.semaphore_wait(barrier, peers)
    for load in loads:
        load.wait()

    parts = xsend.shape[0]
    step = rows // parts
    spans = [(0, 0, rows)] + [(1, i * step, step) for i in range(parts)]

    def xcopy(i):
        span = pl.ds(i * step, step)
        return pltpu.make_async_remote_copy(
            src_ref=nx.at[0, span], dst_ref=nx.at[1, span],
            send_sem=xsend.at[i], recv_sem=xrecv.at[i],
            device_id=(1 - me_x, me), device_id_type=MESH,
        )

    for i in range(parts):
        def norm_step(j, carry, i=i):
            span = pl.ds(pl.multiple_of(i * step + j * 16, 16), 16)
            nx[0, span, :] = normed_rows(tokens[span, :], shift[...], scale[...])
            return carry

        lax.fori_loop(0, step // 16, norm_step, 0)
        xcopy(i).start()

    def chunk(ref, span, p):
        half, low, size = spans[span]
        return ref.at[half, pl.ds(p * PAIR, PAIR), :, pl.ds(low, size)]

    def local(half, p):
        return pltpu.make_async_copy(
            chunk(kv, half, p), chunk(win.at[0], half, p), lsem.at[half, p]
        )

    def remote(half, p, src, dst, target):
        at = half * pairs + p
        source = chunk(kv, half, p) if src == 0 else chunk(win.at[src], half, p)
        return pltpu.make_async_remote_copy(
            src_ref=source, dst_ref=chunk(win.at[dst], half, p),
            send_sem=ssem.at[at, dst], recv_sem=rsem.at[at, dst],
            device_id=target, device_id_type=MESH,
        )

    def along_t(b):
        return [
            (both(ok, has(size_h, at_h, b)), slot(0, b, 0), slot(a, b, 0), device(n, at_h, at_w))
            for a, n, ok in moves(size_t, at_t)
        ]

    def along_h(a):
        return [
            (both(ok, has(size_t, at_t, a)), slot(a, 0, 0), slot(a, b, 0), device(at_t, n, at_w))
            for b, n, ok in moves(size_h, at_h)
        ]

    def along_w(a, b):
        here = both(has(size_t, at_t, a), has(size_h, at_h, b))
        return [
            (both(ok, here), slot(a, b, 0), slot(a, b, c), device(at_t, at_h, n))
            for c, n, ok in moves(size_w, at_w)
        ]

    def start(half, p, sends):
        for ok, src, dst, target in sends:
            guarded(
                ok,
                lambda src=src, dst=dst, target=target: remote(half, p, src, dst, target).start(),
            )

    def await_sent(half, p, sends):
        for ok, src, dst, target in sends:
            guarded(
                ok,
                lambda src=src, dst=dst, target=target: remote(
                    half, p, src, dst, target
                ).wait_send(),
            )

    def await_place(half, p, a, b, c):
        ok = both(both(has(size_t, at_t, a), has(size_h, at_h, b)), has(size_w, at_w, c))
        spot = slot(a, b, c)
        guarded(ok, lambda: remote(half, p, 0, spot, (1 - me_x, me)).wait_recv())

    def time_first(p):
        return p == pairs - 1

    def first(half, p):
        local(half, p).start()
        start(half, p, along_h(0) + along_t(0) + along_w(0, 0))

    def second(half, p):
        for a in range(1, num_t):
            if not time_first(p):
                break
            await_place(half, p, a, 0, 0)
            start(half, p, along_h(a))
        for b in range(1, num_h):
            if time_first(p):
                break
            await_place(half, p, 0, b, 0)
            start(half, p, along_t(b))

    def third(half, p):
        for a in range(num_t):
            for b in range(num_h):
                if a == 0 and b == 0:
                    continue
                waited = (time_first(p) and b == 0) or (not time_first(p) and a == 0)
                if not waited:
                    await_place(half, p, a, b, 0)
                else:
                    continue
                start(half, p, along_w(a, b))

    def early(half, p):
        if time_first(p):
            for a in range(1, num_t):
                start(half, p, along_w(a, 0))
        else:
            for b in range(1, num_h):
                start(half, p, along_w(0, b))

    def finish(half, p):
        for a in range(num_t):
            for b in range(num_h):
                for c in range(1, num_w):
                    await_place(half, p, a, b, c)
        sends = along_t(0) + along_h(0)
        if time_first(p):
            for a in range(1, num_t):
                sends += along_h(a)
        else:
            for b in range(1, num_h):
                sends += along_t(b)
        for a in range(num_t):
            for b in range(num_h):
                sends += along_w(a, b)
        await_sent(half, p, sends)
        local(half, p).wait()

    def project(span, p):
        half, low, size = spans[span]
        at = slice(low, low + size)
        out = jnp.dot(
            nx[half, at], wbuf[p], preferred_element_type=jnp.float32
        ).astype(jnp.bfloat16)
        for i in range(PAIR):
            base = i * 3 * hd
            query = head_norm(out[:, base:base + hd], qgain[...]) * hd ** (-0.5)
            q_out[half, p * PAIR + i, at] = query.astype(jnp.bfloat16)
            key = head_norm(out[:, base + hd:base + 2 * hd], kgain[...])
            kv[half, p * PAIR + i, 0, at] = key.astype(jnp.bfloat16)
            kv[half, p * PAIR + i, 1, at] = out[:, base + 2 * hd:base + 3 * hd]

    for p in range(pairs):
        pltpu.make_async_copy(
            weight.at[:, pl.ds(p * pair_cols, pair_cols)], wbuf.at[p], wsem.at[p]
        ).wait()
        project(0, p)
        first(0, p)
    for p in range(pairs):
        second(0, p)
        early(0, p)
    for i in range(parts):
        xcopy(i).wait_recv()
        for p in range(pairs):
            project(1 + i, p)
            first(1 + i, p)
        if i == 0:
            for p in range(pairs):
                third(0, p)
    for span in range(1, 1 + parts):
        for p in range(pairs):
            second(span, p)
            early(span, p)
        for p in range(pairs):
            third(span, p)
    for span in range(1 + parts):
        for p in range(pairs):
            finish(span, p)
    for i in range(parts):
        xcopy(i).wait_send()


def attend_kernel(
    grid, mask, q_ref, win_ref, weight_hbm, out_ref, att, sbuf, places, count, weight, wsem
):
    head = pl.program_id(0)
    load = pltpu.make_async_copy(weight_hbm, weight, wsem.at[0])

    @pl.when(head == 0)
    def _():
        load.start()
        list_live(grid, mask, places, count)

    q = q_ref[0, 0]
    rows, hd = q.shape
    heads = att.shape[0]
    keys = sbuf.shape[2]
    groups = keys // hd
    trips = (count[0] + 1) // 2

    def both_tiles(i, part):
        return jnp.concatenate(
            [win_ref[places[2 * i + j], half, 0, part] for j in range(2) for half in range(2)],
            axis=0,
        )

    def score(i, top):
        k = both_tiles(i, 0)
        s = lax.dot_general(q, k, (((1,), (1,)), ((), ())), preferred_element_type=jnp.float32)
        ahead, behind = s[:, : keys // 2], s[:, keys // 2:]
        behind = jnp.where(2 * i + 1 < count[0], behind, -1e30)
        sbuf[i, :, : keys // 2] = ahead
        sbuf[i, :, keys // 2:] = behind
        for part in (ahead, behind):
            for g in range(groups // 2):
                top = jnp.maximum(top, part[:, g * hd:(g + 1) * hd])
        return top

    top = lax.fori_loop(0, trips, score, jnp.full((rows, hd), -1e30, jnp.float32))
    top = jnp.max(top, axis=1, keepdims=True)

    def gather(i, carry):
        total, acc = carry
        raised = jnp.exp(sbuf[i] - top)
        for g in range(groups):
            total = total + raised[:, g * hd:(g + 1) * hd]
        acc = acc + jnp.dot(
            raised.astype(jnp.bfloat16), both_tiles(i, 1), preferred_element_type=jnp.float32
        )
        return total, acc

    zero = jnp.zeros((rows, hd), jnp.float32)
    total, acc = lax.fori_loop(0, trips, gather, (zero, zero))
    att[head] = (acc / jnp.sum(total, axis=1, keepdims=True)).astype(jnp.bfloat16)

    @pl.when(head == heads - 1)
    def _():
        load.wait()
        full = jnp.concatenate([att[h] for h in range(heads)], axis=1)
        width = weight.shape[1] // 4
        for i in range(4):
            cols = slice(i * width, (i + 1) * width)
            out_ref[:, cols] = jnp.dot(
                full, weight[:, cols], preferred_element_type=jnp.float32
            ).astype(jnp.bfloat16)


def list_live(grid, mask, places, count):
    size_t, size_h, size_w = grid
    me = lax.axis_index("slab")
    pos = (me // (size_h * size_w), me // size_w % size_h, me % size_w)

    def offsets(size, at):
        return [0, 1 - 2 * at] if size == 2 else [0, -1, 1]

    for i in range(places.shape[0]):
        places[i] = 0
    found = jnp.int32(0)
    spot = 0
    for dt in offsets(size_t, pos[0]):
        for dh in offsets(size_h, pos[1]):
            for dw in offsets(size_w, pos[2]):
                if spot == 0:
                    live = jnp.bool_(True)
                else:
                    live = mask[9 * (dt + 1) + 3 * (dh + 1) + dw + 1] == 1
                    for at, delta, size in zip(pos, (dt, dh, dw), grid):
                        live = live & (at + delta >= 0) & (at + delta < size)

                @pl.when(live)
                def _(found=found, spot=spot):
                    places[found] = spot

                found = found + live.astype(jnp.int32)
                spot += 1
    count[0] = found


def on_device(
    tokens, qkv_weight, out_weight, query_gain, key_gain, mod_shift, mod_scale, branch_gate,
    block_mask,
):
    hd = query_gain.shape[0]
    group_width = out_weight.shape[0]
    heads = group_width // hd
    rows, model = tokens.shape[1:]
    pairs = heads // PAIR
    slab_count = lax.axis_size("slab")
    size_h = min(4, slab_count // 8)
    grid = (GT, size_h, slab_count // (GT * size_h))
    places = slots_of(grid[0]) * slots_of(grid[1]) * slots_of(grid[2])
    vmem = pl.BlockSpec(memory_space=pltpu.VMEM)
    anywhere = pl.BlockSpec(memory_space=pl.ANY)
    bf16 = jnp.bfloat16
    win, queries = pl.pallas_call(
        functools.partial(gather_kernel, grid),
        out_shape=(
            jax.ShapeDtypeStruct((places, 2, heads, 2, rows, hd), bf16),
            jax.ShapeDtypeStruct((2, heads, rows, hd), bf16),
        ),
        in_specs=[pl.BlockSpec(memory_space=pltpu.HBM)] * 6,
        out_specs=(anywhere, vmem),
        scratch_shapes=[
            pltpu.VMEM((rows, model), bf16),
            pltpu.VMEM((1, hd), jnp.float32),
            pltpu.VMEM((1, hd), jnp.float32),
            pltpu.VMEM((1, model), jnp.float32),
            pltpu.VMEM((1, model), jnp.float32),
            pltpu.VMEM((2, rows, model), bf16),
            pltpu.VMEM((pairs, model, 3 * PAIR * hd), bf16),
            pltpu.VMEM((2, heads, 2, rows, hd), bf16),
            pltpu.SemaphoreType.DMA((5,)),
            pltpu.SemaphoreType.DMA((pairs,)),
            pltpu.SemaphoreType.DMA((2,)),
            pltpu.SemaphoreType.DMA((2,)),
            pltpu.SemaphoreType.DMA((3 * pairs, places)),
            pltpu.SemaphoreType.DMA((3 * pairs, places)),
            pltpu.SemaphoreType.DMA((3, pairs)),
        ],
        compiler_params=pltpu.CompilerParams(
            collective_id=0, has_side_effects=True, vmem_limit_bytes=63 * 2**20
        ),
    )(
        tokens[0], qkv_weight, query_gain[None], key_gain[None], mod_shift[None], mod_scale[None]
    )
    trips = (places + 1) // 2

    def attend(half, window):
        return pl.pallas_call(
            functools.partial(attend_kernel, grid),
            grid_spec=pltpu.PrefetchScalarGridSpec(
                num_scalar_prefetch=1,
                grid=(heads,),
                in_specs=[
                    pl.BlockSpec((1, 1, rows, hd), lambda h, *_: (half, h, 0, 0)),
                    pl.BlockSpec((places, 2, 1, 2, rows, hd), lambda h, *_: (0, 0, h, 0, 0, 0)),
                    pl.BlockSpec(memory_space=pltpu.HBM),
                ],
                out_specs=pl.BlockSpec((rows, model), lambda h, *_: (0, 0)),
                scratch_shapes=[
                    pltpu.VMEM((heads, rows, hd), bf16),
                    pltpu.VMEM((trips, rows, 4 * rows), jnp.float32),
                    pltpu.SMEM((places + 2,), jnp.int32),
                    pltpu.SMEM((1,), jnp.int32),
                    pltpu.VMEM(out_weight.shape, bf16),
                    pltpu.SemaphoreType.DMA((1,)),
                ],
            ),
            out_shape=jax.ShapeDtypeStruct((rows, model), bf16),
            compiler_params=pltpu.CompilerParams(vmem_limit_bytes=63 * 2**20),
            cost_estimate=pl.CostEstimate(
                flops=20 * 10**9, bytes_accessed=20 * 10**6, transcendentals=5 * 10**6
            ),
        )(block_mask[0], queries, window, out_weight)

    for_peer = attend(1, win)
    for_peer, later = lax.optimization_barrier((for_peer, win))
    from_peer = lax.ppermute(for_peer, "heads", [(0, 1), (1, 0)])
    own = attend(0, later)
    summed = own.astype(jnp.float32) + from_peer.astype(jnp.float32)
    return (branch_gate * summed).astype(bf16)[None]


def solution(mesh):
    in_specs = (
        P("slab", "heads", None),
        P(None, "heads"),
        P("heads", None),
        P(),
        P(),
        P(),
        P(),
        P(),
        P("slab", None),
    )
    return jax.shard_map(
        on_device, mesh=mesh, in_specs=in_specs, out_specs=P("slab", "heads", None),
        check_vma=False,
    )
```
